32 devices in a mesh: groups: 2 (over y), tensor: 8 (over z, x), dp: 2 (over core).
Axes of the slice: x: 2, y: 2, z: 4, core: 2. Of those that a mesh axis runs over, the one named last changes fastest.
Arguments:
- x_act: bfloat16 [3072, 8192], P(('groups', 'dp'), 'tensor'), parts along dimension 0, may hold values from -6 to 6
- gate_pre: bfloat16 [3072, 28672], P(('groups', 'dp'), 'tensor'), parts along dimension 0, may hold values from -6 to 6
- up_pre: bfloat16 [3072, 28672], P(('groups', 'dp'), 'tensor'), parts along dimension 0, may hold values from -6 to 6
- out_grad: bfloat16 [3072, 8192], P(('groups', 'dp'), 'tensor'), parts along dimension 0, may hold values from -6 to 6
- down_weight: bfloat16 [28672, 8192], P('tensor'), may hold values from -0.0625 to 0.0625
- proj_input: bfloat16 [8192, 64], P('tensor'), may hold values from -0.0625 to 0.0625
- proj_gate: bfloat16 [28672, 64], P('tensor'), may hold values from -0.03125 to 0.03125
- proj_up: bfloat16 [28672, 64], P('tensor'), may hold values from -0.03125 to 0.03125
- proj_hidden: bfloat16 [28672, 64], P('tensor'), may hold values from -0.03125 to 0.03125
- proj_output: bfloat16 [8192, 64], P('tensor'), may hold values from -0.0625 to 0.0625
- target_sketch: bfloat16 [512, 12288], P(('groups', 'tensor')), parts along dimension 0, may hold values from -6 to 6
- token_ids: int32 [16, 192], P(('groups', 'dp')), parts along dimension 0, may hold values from 0 to 128255, as said below
- source_label: int32 [16], P(('groups', 'dp')), parts along dimension 0, may hold values from 0 to 3
Outputs:
- scores: float32 [16, 256], P(('groups', 'dp'), 'tensor'), parts along dimension 0
- source_scores: float32 [8, 256], P('groups', 'tensor'), parts along dimension 0
The draws below stay inside these ranges and needn't reach their ends.
There are 2 independent parts, one for each index of `groups`. The reference program is written for one: setup_inputs(seed, part) draws one part's arguments, and reference() takes and returns one part's arrays. A program takes and returns all parts, laid end to end along the dimension named above; an argument that names none is the same for every part. Nothing has to cross between parts.
Inputs may be any that keep to these rules, and one draw needn't show every extreme that they name: `token_ids`: each candidate's ids are non-zero ids followed by padding zeros; its first 96 ids are non-zero, the first candidate has no padding, and the last has exactly 96 non-zero ids.
All inputs are finite; a program needn't handle non-finite values.
Results may differ from the reference program's by a relative error of at most 0.003.
Values may be sent and summed in bfloat16 or wider, within the bound.
A program may use at most 192 MiB of HBM per device.

```python
import jax
import jax.numpy as jnp
from jax import lax

D = 8192
FF = 28672
VOCAB = 128256
R = 64
SEQ_LEN = 192
NSRC = 4
NCAND = 8
TOKENS = 1536
NT = 256


def draw_token_ids(key, part):
    key = jax.random.fold_in(key, 11)
    key_len, key_ids = jax.random.split(key)
    lengths = jax.random.randint(key_len, (NCAND,), SEQ_LEN // 2, SEQ_LEN + 1)
    lengths = lengths.at[0].set(SEQ_LEN)
    lengths = lengths.at[NCAND - 1].set(SEQ_LEN // 2)
    ids = jax.random.randint(key_ids, (NCAND, SEQ_LEN), 1, VOCAB)
    ids = ids.at[0, 0].set(VOCAB - 1)
    positions = jnp.arange(SEQ_LEN)[None, :]
    return jnp.where(positions < lengths[:, None], ids, 0).astype(jnp.int32)


def plant(drawn, stream_key, smallest, largest):
    longest = drawn.shape.index(max(drawn.shape))
    spots = []
    for shift in (0, 1):
        where = [jax.random.randint(jax.random.fold_in(stream_key, axis), (), 0, length) for axis, length in enumerate(drawn.shape)]
        where[longest] = (where[longest] + shift) % drawn.shape[longest]
        spots.append(tuple(where))
    return drawn.at[spots[0]].set(smallest).at[spots[1]].set(largest)


def steps_of(stream_key, dims, pieces, least, top_value):
    loudness, own = 1.0, jax.random.fold_in(stream_key, 6)
    for dim, parts in pieces:
        steps = jnp.exp(jax.random.uniform(jax.random.fold_in(own, dim), (parts,), jnp.float32, least / len(pieces), top_value / len(pieces)))
        loudness = loudness * jnp.repeat(steps, dims[dim] // parts).reshape([-1 if axis == dim else 1 for axis in range(len(dims))])
    return loudness


def bell_draw(rng, extent, width, bound, shards=(), held_as=jnp.bfloat16):
    loudness = steps_of(rng, extent, shards, -0.22, 0.18) if shards else 1.0
    entries = jax.random.normal(rng, extent, jnp.float32) * width * loudness
    return jnp.minimum(jnp.maximum(entries, -bound), bound).astype(held_as)


def setup_inputs(seed: int = 0, part: int = 0) -> dict:
    arg_keys = jax.random.split(jax.random.key(seed), 14)
    own_keys = jax.random.split(jax.random.fold_in(arg_keys[13], part), 14)
    x_act = bell_draw(own_keys[0], (TOKENS, D), 1.0, 6.0, ((0, 2), (1, 8)))
    gate_pre = bell_draw(own_keys[1], (TOKENS, FF), 1.0, 6.0, ((0, 2), (1, 8)))
    up_pre = bell_draw(own_keys[2], (TOKENS, FF), 1.0, 6.0, ((0, 2), (1, 8)))
    out_grad = bell_draw(own_keys[3], (TOKENS, D), 1.0, 6.0, ((0, 2), (1, 8)))
    down_weight = bell_draw(arg_keys[4], (FF, D), D ** -0.5, 0.0625, ((0, 8),))
    proj_input = bell_draw(arg_keys[5], (D, R), D ** -0.5, 0.0625, ((0, 8),))
    proj_gate = bell_draw(arg_keys[6], (FF, R), FF ** -0.5, 0.03125, ((0, 8),))
    proj_up = bell_draw(arg_keys[7], (FF, R), FF ** -0.5, 0.03125, ((0, 8),))
    proj_hidden = bell_draw(arg_keys[8], (FF, R), FF ** -0.5, 0.03125, ((0, 8),))
    proj_output = bell_draw(arg_keys[9], (D, R), D ** -0.5, 0.0625, ((0, 8),))
    target_sketch = bell_draw(own_keys[10], (NT, 3 * R * R), 1.0, 6.0, ((0, 8),))
    token_ids = draw_token_ids(jax.random.fold_in(jax.random.fold_in(arg_keys[13], part), 71), part)
    source_label = plant(jax.random.randint(own_keys[12], (NCAND,), 0, NSRC), jax.random.fold_in(own_keys[12], 1), 0, NSRC - 1).astype(jnp.int32)
    return dict(x_act=x_act, gate_pre=gate_pre, up_pre=up_pre, out_grad=out_grad, down_weight=down_weight, proj_input=proj_input, proj_gate=proj_gate, proj_up=proj_up, proj_hidden=proj_hidden, proj_output=proj_output, target_sketch=target_sketch, token_ids=token_ids, source_label=source_label)


def dotf(left, right):
    return jnp.dot(left, right, preferred_element_type=jnp.float32)

def reference(x_act, gate_pre, up_pre, out_grad, down_weight, proj_input, proj_gate, proj_up, proj_hidden, proj_output, target_sketch, token_ids, source_label):
    grad_hidden = lax.dot_general(out_grad, down_weight, (((1,), (1,)), ((), ())), preferred_element_type=jnp.float32)
    gval = gate_pre.astype(jnp.float32)
    uval = up_pre.astype(jnp.float32)
    sig = jax.nn.sigmoid(gval)
    hidden = (gval * sig * uval).astype(jnp.bfloat16)
    grad_gate = (grad_hidden * uval * sig * (1.0 + gval * (1.0 - sig))).astype(jnp.bfloat16)
    grad_up = (grad_hidden * gval * sig).astype(jnp.bfloat16)
    mask = (token_ids != 0).astype(jnp.float32).reshape(-1)[:, None]
    p_in = (dotf(x_act, proj_input) * mask).reshape(NCAND, SEQ_LEN, R)
    p_gate = dotf(grad_gate, proj_gate).reshape(NCAND, SEQ_LEN, R)
    p_up = dotf(grad_up, proj_up).reshape(NCAND, SEQ_LEN, R)
    p_hid = (dotf(hidden, proj_hidden) * mask).reshape(NCAND, SEQ_LEN, R)
    p_out = dotf(out_grad, proj_output).reshape(NCAND, SEQ_LEN, R)
    hp = lax.Precision.HIGHEST
    first = jnp.einsum('csi,csj->cij', p_in, p_gate, precision=hp)
    second = jnp.einsum('csi,csj->cij', p_in, p_up, precision=hp)
    third = jnp.einsum('csi,csj->cij', p_hid, p_out, precision=hp)
    sketch = jnp.concatenate([first.reshape(NCAND, R * R), second.reshape(NCAND, R * R), third.reshape(NCAND, R * R)], axis=1)
    inv_norm = lax.rsqrt(lax.optimization_barrier(jnp.mean(sketch * sketch, axis=1, keepdims=True)) + 1e-06)
    unit = sketch * inv_norm
    scores = jnp.dot(unit, target_sketch.astype(jnp.float32).T, precision=hp) / jnp.sqrt(jnp.float32(3 * R * R))
    onehot = (source_label[:, None] == jnp.arange(NSRC, dtype=jnp.int32)[None, :]).astype(jnp.float32)
    totals = jnp.dot(onehot.T, scores, precision=hp)
    counts = lax.optimization_barrier(jnp.sum(onehot, axis=0))
    source_scores = totals / jnp.maximum(counts, 1.0)[:, None]
    return (scores, source_scores)
```

```python
import functools

import jax
import jax.numpy as jnp
from jax import lax
from jax.experimental import pallas as pl
from jax.experimental.pallas import tpu as pltpu
from jax.sharding import PartitionSpec as P

NSRC = 4
MESH = pl.DeviceIdType.MESH
F32 = jnp.float32
BF16 = jnp.bfloat16
TILE = 256


def dotf(left, right):
    return jnp.dot(left, right, preferred_element_type=jnp.float32)


def dot_nt(left, right):
    return lax.dot_general(left, right, (((1,), (1,)), ((), ())), preferred_element_type=F32)


def dot_tn(left, right):
    return lax.dot_general(
        left, right, (((0,), (0,)), ((), ())), preferred_element_type=F32, precision=lax.Precision.HIGHEST
    )


def fused_kernel(
    x_hbm, g_hbm, u_hbm, og_hbm, w_hbm, pi_hbm, pg_hbm, pu_hbm, ph_hbm, po_hbm, mask_ref,
    out_ref,
    gath, acc, fa, fb, wbuf, gbuf, ubuf, pi, pg, pu, ph, po, hid_acc, gate_acc, up_acc,
    send0, send1, red0, red1, sk,
    s_send, s_recv, s_own, s_w, s_x, s_g, s_u, s_p, s_rs, s_rr, s_ss, s_sr,
):
    rows, half = gath.shape[1], gath.shape[2]
    ff = acc.shape[1]
    tiles = ff // TILE
    n = 8
    part = rows // n
    me = lax.axis_index("tensor")
    col, z = me % 2, me // 2
    other = 1 - col
    flip = z // 2
    pos = z + flip * (3 - 2 * z)

    def plane(v):
        return v + flip * (3 - 2 * v)

    def tid(c, v):
        return plane(v) * 2 + c

    near, mid, far = 1 - pos, 2, 3
    to_x, to_near, to_up = tid(other, pos), tid(col, near), tid(col, mid)

    own_copies = [
        pltpu.make_async_copy(
            og_hbm.at[:, pl.ds(h * half, half)], gath.at[2 * me + h], s_own.at[h]
        )
        for h in range(2)
    ]
    for c in own_copies:
        c.start()

    def w_copy(slot, k):
        return pltpu.make_async_copy(
            w_hbm.at[:, pl.ds(pl.multiple_of(slot * half, half), half)], wbuf.at[k], s_w.at[k]
        )

    small = [
        pltpu.make_async_copy(src, dst, s_p.at[i])
        for i, (src, dst) in enumerate(
            ((pi_hbm, pi), (ph_hbm, ph), (po_hbm, po), (pg_hbm, pg), (pu_hbm, pu))
        )
    ]
    x_copies = [
        pltpu.make_async_copy(
            x_hbm.at[:, pl.ds(h * half, half)], wbuf.at[1, pl.ds(h * rows, rows)], s_x.at[h]
        )
        for h in range(2)
    ]

    barrier = pltpu.get_barrier_semaphore()
    for d in range(1, n):
        pl.semaphore_signal(
            barrier, inc=1, device_id={"tensor": (me + d) % n}, device_id_type=MESH
        )
    pl.semaphore_wait(barrier, n - 1)

    def piece(slot, way, target):
        return pltpu.make_async_remote_copy(
            src_ref=gath.at[slot], dst_ref=gath.at[slot],
            send_sem=s_send.at[slot, way], recv_sem=s_recv.at[slot],
            device_id={"tensor": target}, device_id_type=MESH,
        )

    def go_x(slot):
        piece(slot, 0, to_x).start()

    def go_near(slot):
        piece(slot, 1, to_near).start()

    def go_up(slot):
        piece(slot, 2, to_up).start()

    own = [2 * me, 2 * me + 1]
    xo = [2 * to_x, 2 * to_x + 1]
    a = [2 * tid(col, near) + h for h in range(2)]
    b = [2 * tid(col, mid) + h for h in range(2)]
    c = [2 * tid(col, far) + h for h in range(2)]
    xa = [2 * tid(other, near) + h for h in range(2)]
    xb = [2 * tid(other, mid) + h for h in range(2)]
    xc = [2 * tid(other, far) + h for h in range(2)]
    at1 = pos == 1

    own_copies[0].wait()
    go_x(own[0])
    go_near(own[0])

    @pl.when(at1)
    def _():
        go_up(own[0])

    w_copy(own[0], 0).start()
    for cp in small + x_copies:
        cp.start()

    def gu_copies(j, k):
        cols = pl.ds(pl.multiple_of(j * TILE, TILE), TILE)
        return (
            pltpu.make_async_copy(g_hbm.at[:, cols], gbuf.at[k], s_g.at[k]),
            pltpu.make_async_copy(u_hbm.at[:, cols], ubuf.at[k], s_u.at[k]),
        )

    for cp in gu_copies(0, 0):
        cp.start()
    hid_acc[...] = jnp.zeros_like(hid_acc)
    gate_acc[...] = jnp.zeros_like(gate_acc)
    up_acc[...] = jnp.zeros_like(up_acc)
    for cp in small:
        cp.wait()
    chunk = rows // 6

    def factors(j, carry):
        k = j % 2

        @pl.when(j + 1 < tiles)
        def _():
            for cp in gu_copies(j + 1, 1 - k):
                cp.start()

        for cp in gu_copies(j, k):
            cp.wait()
        base = pl.multiple_of(j * TILE, TILE)

        def rows_of(r, carry2):
            rs = pl.ds(pl.multiple_of(r * chunk, chunk), chunk)
            g = gbuf[k, rs, :].astype(F32)
            u = ubuf[k, rs, :].astype(F32)
            s = jax.nn.sigmoid(g)
            gs = g * s
            fb[rs, pl.ds(base, TILE)] = gs
            fa[rs, pl.ds(base, TILE)] = u * s * (1.0 + g * (1.0 - s))
            hidden = (gs * u).astype(BF16)
            hid_acc[rs, :] += dotf(hidden, ph[pl.ds(base, TILE), :])
            return carry2

        return lax.fori_loop(0, 6, rows_of, carry)

    lax.fori_loop(0, tiles // 2, factors, 0)

    own_copies[1].wait()
    go_x(own[1])
    go_near(own[1])

    @pl.when(at1)
    def _():
        go_up(own[1])

    lax.fori_loop(tiles // 2, tiles, factors, 0)

    for cp in x_copies:
        cp.wait()
    pin = dotf(wbuf[1, 0:rows, :], pi[0:half, :]) + dotf(
        wbuf[1, rows : 2 * rows, :], pi[half : 2 * half, :]
    )
    send0[:, 0:128] = jnp.concatenate(
        [
            pin,
            dotf(gath[own[0]], po[0:half, :]) + dotf(gath[own[1]], po[half : 2 * half, :]),
        ],
        axis=1,
    )
    send0[:, 128:256] = jnp.concatenate([hid_acc[...], jnp.zeros((rows, 64), F32)], axis=1)

    def tile_of(j):
        return pl.ds(pl.multiple_of(j * TILE, TILE), TILE)

    def matmul(slot, k, first):
        def body(j, carry):
            prod = dot_nt(gath[slot], wbuf[k, tile_of(j), :])
            if first:
                acc[:, tile_of(j)] = prod
            else:
                acc[:, tile_of(j)] += prod
            return carry

        lax.fori_loop(0, tiles, body, 0)

    def last(slot, k):
        def body(j, carry):
            gh = acc[:, tile_of(j)] + dot_nt(gath[slot], wbuf[k, tile_of(j), :])
            gg = (gh * fa[:, tile_of(j)]).astype(BF16)
            gu = (gh * fb[:, tile_of(j)]).astype(BF16)
            gate_acc[...] += dotf(gg, pg[tile_of(j), :])
            up_acc[...] += dotf(gu, pu[tile_of(j), :])
            return carry

        lax.fori_loop(0, tiles, body, 0)

    def reduce_copy(i, src, dst, target, source):
        return pltpu.make_async_remote_copy(
            src_ref=src.at[pl.ds(pl.multiple_of(target * part, part), part)],
            dst_ref=dst.at[source],
            send_sem=s_rs.at[i, target], recv_sem=s_rr.at[i, source],
            device_id={"tensor": target}, device_id_type=MESH,
        )

    def nothing():
        pass

    def f_xo1():
        @pl.when(pos == 0)
        def _():
            go_near(xo[1])

    def f_a0():
        go_x(a[0])

        @pl.when(at1)
        def _():
            go_up(a[0])

    def f_a1():
        @pl.when(at1)
        def _():
            go_up(a[1])

    def f_b0():
        go_x(b[0])

        @pl.when(at1)
        def _():
            go_near(b[0])

    def f_b1():
        @pl.when(at1)
        def _():
            go_near(b[1])

        @pl.when(pos == 0)
        def _():
            go_x(b[1])

    def f_c0():
        go_x(c[0])

        @pl.when(at1)
        def _():
            go_near(c[0])

    def f_c1():
        go_x(c[1])

        @pl.when(at1)
        def _():
            go_near(c[1])
            go_near(xo[1])
            go_up(xo[1])

    def f_last():
        for d in range(1, n):
            reduce_copy(0, send0, red0, (me + d) % n, me).start()

    order = [
        (own[0], None), (own[1], None),
        (xo[0], nothing), (a[0], f_a0), (xo[1], f_xo1), (a[1], f_a1), (b[0], f_b0),
        (xa[0], nothing), (b[1], f_b1), (c[0], f_c0), (xb[0], nothing), (c[1], f_c1),
        (xb[1], nothing), (xc[0], nothing), (xa[1], nothing), (xc[1], f_last),
    ]
    steps = len(order)
    for i, (slot, forward) in enumerate(order):
        if i + 1 < steps:
            w_copy(order[i + 1][0], (i + 1) % 2).start()
        if forward is not None:
            piece(slot, 0, to_x).wait_recv()
            forward()
        w_copy(slot, i % 2).wait()
        if i + 1 < steps:
            matmul(slot, i % 2, i == 0)
        else:
            last(slot, i % 2)

    send1[...] = jnp.concatenate([gate_acc[...], up_acc[...]], axis=1)
    for d in range(1, n):
        reduce_copy(1, send1, red1, (me + d) % n, me).start()
    mine = pl.ds(pl.multiple_of(me * part, part), part)
    sum0, sum1 = send0[mine, :], send1[mine, :]
    for d in range(1, n):
        src = (me + d) % n
        reduce_copy(0, send0, red0, src, src).wait_recv()
        sum0 = sum0 + red0[src]
    for d in range(1, n):
        src = (me + d) % n
        reduce_copy(1, send1, red1, src, src).wait_recv()
        sum1 = sum1 + red1[src]
    masked = sum0 * mask_ref[mine, :]
    sk[me, 0:64, :] = dot_tn(masked[:, 0:64], sum1)
    sk[me, 64:128, :] = dot_tn(masked[:, 128:192], sum0[:, 0:128])

    def sketch_copy(target, source):
        return pltpu.make_async_remote_copy(
            src_ref=sk.at[source], dst_ref=sk.at[source],
            send_sem=s_ss.at[target], recv_sem=s_sr.at[source],
            device_id={"tensor": target}, device_id_type=MESH,
        )

    for d in range(1, n):
        sketch_copy((me + d) % n, me).start()
    for slot in own + [a[0], c[0], c[1], b[0]]:
        piece(slot, 0, to_x).wait_send()
    for slot in own:
        piece(slot, 1, to_near).wait_send()

    @pl.when(pos == 0)
    def _():
        piece(b[1], 0, to_x).wait_send()
        piece(xo[1], 1, to_near).wait_send()

    @pl.when(at1)
    def _():
        for slot in own + [a[0], a[1], xo[1]]:
            piece(slot, 2, to_up).wait_send()
        for slot in [b[0], b[1], c[0], c[1], xo[1]]:
            piece(slot, 1, to_near).wait_send()

    for d in range(1, n):
        t = (me + d) % n
        reduce_copy(0, send0, red0, t, me).wait_send()
        reduce_copy(1, send1, red1, t, me).wait_send()
    for d in range(1, n):
        t = (me + d) % n
        sketch_copy(t, t).wait_recv()
    for d in range(1, n):
        sketch_copy((me + d) % n, me).wait_send()
    out_ref[...] = sk[...]


def fused(x_act, gate_pre, up_pre, out_grad, down_weight, pi, pg, pu, ph, po, mask):
    rows, feat = x_act.shape
    ff = gate_pre.shape[1]
    half = feat // 2
    n = 8
    rank = pi.shape[1]
    part = rows // n
    dma = pltpu.SemaphoreType.DMA
    vm = pltpu.VMEM
    any_spec = pl.BlockSpec(memory_space=pl.ANY)
    return pl.pallas_call(
        fused_kernel,
        out_shape=jax.ShapeDtypeStruct((n, 2 * rank, 2 * rank), F32),
        in_specs=[any_spec] * 10 + [pl.BlockSpec(memory_space=pltpu.VMEM)],
        out_specs=pl.BlockSpec(memory_space=pltpu.VMEM),
        scratch_shapes=[
            vm((2 * n, rows, half), BF16),
            vm((rows, ff), F32),
            vm((rows, ff), F32),
            vm((rows, ff), F32),
            vm((2, ff, half), BF16),
            vm((2, rows, TILE), BF16),
            vm((2, rows, TILE), BF16),
            vm((feat, rank), BF16),
            vm((ff, rank), BF16),
            vm((ff, rank), BF16),
            vm((ff, rank), BF16),
            vm((feat, rank), BF16),
            vm((rows, rank), F32),
            vm((rows, rank), F32),
            vm((rows, rank), F32),
            vm((rows, 4 * rank), F32),
            vm((rows, 2 * rank), F32),
            vm((n, part, 4 * rank), F32),
            vm((n, part, 2 * rank), F32),
            vm((n, 2 * rank, 2 * rank), F32),
            dma((2 * n, 3)), dma((2 * n,)), dma((2,)), dma((2,)), dma((2,)), dma((2,)), dma((2,)),
            dma((5,)), dma((2, n)), dma((2, n)), dma((n,)), dma((n,)),
        ],
        compiler_params=pltpu.CompilerParams(
            collective_id=0, has_side_effects=True, vmem_limit_bytes=VLIM
        ),
        cost_estimate=pl.CostEstimate(
            flops=2 * rows * ff * feat * n, bytes_accessed=2 * ff * feat * n, transcendentals=rows * ff
        ),
    )(x_act, gate_pre, up_pre, out_grad, down_weight, pi, pg, pu, ph, po, mask)


VLIM = 66 * 1000 * 1000


def tail(sketch, target_sketch, source_label):
    highest = lax.Precision.HIGHEST
    inv_norm = lax.rsqrt(jnp.mean(sketch * sketch, axis=1, keepdims=True) + 1e-06)
    unit = sketch * inv_norm
    scores = jnp.dot(unit, target_sketch.astype(F32).T, precision=highest) / jnp.sqrt(
        F32(sketch.shape[1])
    )
    onehot = (source_label[:, None] == jnp.arange(NSRC, dtype=jnp.int32)[None, :]).astype(F32)
    local_totals = jnp.dot(onehot.T, scores, precision=highest)
    local_counts = jnp.sum(onehot, axis=0)
    totals, counts = lax.psum((local_totals, local_counts), "dp")
    source_scores = totals / jnp.maximum(counts, 1.0)[:, None]
    return (scores, source_scores)


def local_fused(
    x_act, gate_pre, up_pre, out_grad, down_weight, proj_input, proj_gate, proj_up, proj_hidden,
    proj_output, target_sketch, token_ids, source_label,
):
    rows = x_act.shape[0]
    cands = token_ids.shape[0]
    r = proj_input.shape[1]
    mask = (token_ids != 0).astype(F32).reshape(rows, 1)
    parts = fused(
        x_act, gate_pre, up_pre, out_grad, down_weight,
        proj_input, proj_gate, proj_up, proj_hidden, proj_output, mask,
    )
    mats = parts.reshape(cands, 8 // cands, 2 * r, 2 * r).sum(axis=1)
    sketch = jnp.concatenate(
        [
            mats[:, :r, :r].reshape(cands, r * r),
            mats[:, :r, r:].reshape(cands, r * r),
            mats[:, r:, r:].reshape(cands, r * r),
        ],
        axis=1,
    )
    return tail(sketch, target_sketch, source_label)


def local(
    x_act,
    gate_pre,
    up_pre,
    out_grad,
    down_weight,
    proj_input,
    proj_gate,
    proj_up,
    proj_hidden,
    proj_output,
    target_sketch,
    token_ids,
    source_label,
):
    tok_rows = x_act.shape[0]
    cands, seq_len = token_ids.shape
    rank = proj_input.shape[1]
    highest = lax.Precision.HIGHEST
    grad_hidden = lax.dot_general(
        lax.all_gather(out_grad, "tensor", axis=1, tiled=True),
        down_weight,
        (((1,), (1,)), ((), ())),
        preferred_element_type=jnp.float32,
    )
    gval = gate_pre.astype(jnp.float32)
    uval = up_pre.astype(jnp.float32)
    sig = jax.nn.sigmoid(gval)
    hidden = (gval * sig * uval).astype(jnp.bfloat16)
    grad_gate = (grad_hidden * uval * sig * (1.0 + gval * (1.0 - sig))).astype(jnp.bfloat16)
    grad_up = (grad_hidden * gval * sig).astype(jnp.bfloat16)
    mask = (token_ids != 0).astype(jnp.float32).reshape(tok_rows)
    term_in = dotf(x_act, proj_input)
    term_gate = dotf(grad_gate, proj_gate)
    term_up = dotf(grad_up, proj_up)
    term_hid = dotf(hidden, proj_hidden)
    term_out = dotf(out_grad, proj_output)
    whole = lax.psum((term_in, term_gate, term_up, term_hid, term_out), "tensor")
    p_in = (whole[0] * mask[:, None]).reshape(cands, seq_len, rank)
    p_gate = whole[1].reshape(cands, seq_len, rank)
    p_up = whole[2].reshape(cands, seq_len, rank)
    p_hid = (whole[3] * mask[:, None]).reshape(cands, seq_len, rank)
    p_out = whole[4].reshape(cands, seq_len, rank)
    first = jnp.einsum("csi,csj->cij", p_in, p_gate, precision=highest)
    second = jnp.einsum("csi,csj->cij", p_in, p_up, precision=highest)
    third = jnp.einsum("csi,csj->cij", p_hid, p_out, precision=highest)
    sketch = jnp.concatenate(
        [
            first.reshape(cands, rank * rank),
            second.reshape(cands, rank * rank),
            third.reshape(cands, rank * rank),
        ],
        axis=1,
    )
    return tail(sketch, target_sketch, source_label)


def solution(mesh):
    in_specs = (
        P(("groups", "dp"), "tensor"),
        P(("groups", "dp"), "tensor"),
        P(("groups", "dp"), "tensor"),
        P(("groups", "dp"), "tensor"),
        P("tensor", None),
        P("tensor", None),
        P("tensor", None),
        P("tensor", None),
        P("tensor", None),
        P("tensor", None),
        P(("groups", "tensor"), None),
        P(("groups", "dp"), None),
        P(("groups", "dp")),
    )
    out_specs = (P(("groups", "dp"), "tensor"), P("groups", "tensor"))
    body = local_fused if mesh.shape["tensor"] == 8 else local
    return jax.shard_map(body, mesh=mesh, in_specs=in_specs, out_specs=out_specs, check_vma=False)
```

```python
import functools

import jax
import jax.numpy as jnp
from jax import lax
from jax.experimental import pallas as pl
from jax.experimental.pallas import tpu as pltpu
from jax.sharding import PartitionSpec as P

NSRC = 4
MESH = pl.DeviceIdType.MESH
F32 = jnp.float32
BF16 = jnp.bfloat16
TILE = 256
WIDE = 1792
TAIL = 512


def dotf(left, right):
    return jnp.dot(left, right, preferred_element_type=jnp.float32)


def dot_nt(left, right):
    return lax.dot_general(left, right, (((1,), (1,)), ((), ())), preferred_element_type=F32)


def dot_tn(left, right):
    return lax.dot_general(
        left, right, (((0,), (0,)), ((), ())), preferred_element_type=F32, precision=lax.Precision.HIGHEST
    )


def fused_kernel(
    x_hbm, g_hbm, u_hbm, og_hbm, w_hbm, pi_hbm, pg_hbm, pu_hbm, ph_hbm, po_hbm, ids_ref,
    out_ref,
    gath, acc, fa, fb, wbuf, gbuf, ubuf, pi, pg, pu, ph, po, hid_acc, gate_acc, up_acc,
    send0, send1, red0, red1, sk,
    s_send, s_recv, s_own, s_w, s_x, s_g, s_u, s_p, s_rs, s_rr, s_ss, s_sr,
):
    rows, half = gath.shape[1], gath.shape[2]
    ff = acc.shape[1]
    tiles = ff // TILE
    n = 8
    part = rows // n
    me = lax.axis_index("tensor")
    col, z = me % 2, me // 2
    other = 1 - col
    flip = z // 2
    pos = z + flip * (3 - 2 * z)

    def plane(v):
        return v + flip * (3 - 2 * v)

    def tid(c, v):
        return plane(v) * 2 + c

    near, mid, far = 1 - pos, 2, 3
    to_x, to_near, to_up = tid(other, pos), tid(col, near), tid(col, mid)

    own_copies = [
        pltpu.make_async_copy(
            og_hbm.at[:, pl.ds(h * half, half)], gath.at[2 * me + h], s_own.at[h]
        )
        for h in range(2)
    ]
    for c in own_copies:
        c.start()

    def w_copy(slot, k):
        return pltpu.make_async_copy(
            w_hbm.at[:, pl.ds(pl.multiple_of(slot * half, half), half)], wbuf.at[k], s_w.at[k]
        )

    small = [
        pltpu.make_async_copy(src, dst, s_p.at[i])
        for i, (src, dst) in enumerate(
            ((pi_hbm, pi), (ph_hbm, ph), (po_hbm, po), (pg_hbm, pg), (pu_hbm, pu))
        )
    ]
    x_copies = [
        pltpu.make_async_copy(
            x_hbm.at[:, pl.ds(h * half, half)], wbuf.at[1, pl.ds(h * rows, rows)], s_x.at[h]
        )
        for h in range(2)
    ]

    barrier = pltpu.get_barrier_semaphore()
    for d in range(1, n):
        pl.semaphore_signal(
            barrier, inc=1, device_id={"tensor": (me + d) % n}, device_id_type=MESH
        )
    pl.semaphore_wait(barrier, n - 1)

    def piece(slot, way, target):
        return pltpu.make_async_remote_copy(
            src_ref=gath.at[slot], dst_ref=gath.at[slot],
            send_sem=s_send.at[slot, way], recv_sem=s_recv.at[slot],
            device_id={"tensor": target}, device_id_type=MESH,
        )

    def go_x(slot):
        piece(slot, 0, to_x).start()

    def go_near(slot):
        piece(slot, 1, to_near).start()

    def go_up(slot):
        piece(slot, 2, to_up).start()

    own = [2 * me, 2 * me + 1]
    xo = [2 * to_x, 2 * to_x + 1]
    a = [2 * tid(col, near) + h for h in range(2)]
    b = [2 * tid(col, mid) + h for h in range(2)]
    c = [2 * tid(col, far) + h for h in range(2)]
    xa = [2 * tid(other, near) + h for h in range(2)]
    xb = [2 * tid(other, mid) + h for h in range(2)]
    xc = [2 * tid(other, far) + h for h in range(2)]
    at1 = pos == 1

    own_copies[0].wait()
    go_x(own[0])
    go_near(own[0])

    @pl.when(at1)
    def _():
        go_up(own[0])

    w_copy(own[0], 0).start()
    for cp in small + x_copies:
        cp.start()

    def gu_copies(j, k):
        cols = pl.ds(pl.multiple_of(j * TILE, TILE), TILE)
        return (
            pltpu.make_async_copy(g_hbm.at[:, cols], gbuf.at[k], s_g.at[k]),
            pltpu.make_async_copy(u_hbm.at[:, cols], ubuf.at[k], s_u.at[k]),
        )

    for cp in gu_copies(0, 0):
        cp.start()
    hid_acc[...] = jnp.zeros_like(hid_acc)
    gate_acc[...] = jnp.zeros_like(gate_acc)
    up_acc[...] = jnp.zeros_like(up_acc)
    for cp in small:
        cp.wait()
    chunk = rows // 6

    def factors(j, carry):
        k = j % 2

        @pl.when(j + 1 < tiles)
        def _():
            for cp in gu_copies(j + 1, 1 - k):
                cp.start()

        for cp in gu_copies(j, k):
            cp.wait()
        base = pl.multiple_of(j * TILE, TILE)

        def rows_of(r, carry2):
            rs = pl.ds(pl.multiple_of(r * chunk, chunk), chunk)
            g = gbuf[k, rs, :].astype(F32)
            u = ubuf[k, rs, :].astype(F32)
            s = jax.nn.sigmoid(g)
            gs = g * s
            fb[rs, pl.ds(base, TILE)] = gs
            fa[rs, pl.ds(base, TILE)] = u * s * (1.0 + g * (1.0 - s))
            hidden = (gs * u).astype(BF16)
            hid_acc[rs, :] += dot_nt(hidden, ph[:, pl.ds(base, TILE)])
            return carry2

        return lax.fori_loop(0, 6, rows_of, carry)

    lax.fori_loop(0, tiles // 2, factors, 0)

    own_copies[1].wait()
    go_x(own[1])
    go_near(own[1])

    @pl.when(at1)
    def _():
        go_up(own[1])

    lax.fori_loop(tiles // 2, tiles, factors, 0)

    for cp in x_copies:
        cp.wait()
    pin = dot_nt(wbuf[1, 0:rows, :], pi[:, 0:half]) + dot_nt(
        wbuf[1, rows : 2 * rows, :], pi[:, half : 2 * half]
    )
    send0[:, 0:128] = jnp.concatenate(
        [
            pin,
            dot_nt(gath[own[0]], po[:, 0:half]) + dot_nt(gath[own[1]], po[:, half : 2 * half]),
        ],
        axis=1,
    )
    send0[:, 128:256] = jnp.concatenate([hid_acc[...], jnp.zeros((rows, 64), F32)], axis=1)

    def wide(j):
        return pl.ds(pl.multiple_of(j * WIDE, WIDE), WIDE)

    def tail_of(j):
        return pl.ds(pl.multiple_of(j * TAIL, TAIL), TAIL)

    def matmul(slot, k, first):
        def body(j, carry):
            prod = dot_nt(gath[slot], wbuf[k, wide(j), :])
            if first:
                acc[:, wide(j)] = prod
            else:
                acc[:, wide(j)] += prod
            return carry

        lax.fori_loop(0, ff // WIDE, body, 0)

    def last(slot, k):
        def body(j, carry):
            gh = acc[:, tail_of(j)] + dot_nt(gath[slot], wbuf[k, tail_of(j), :])
            gg = (gh * fa[:, tail_of(j)]).astype(BF16)
            gu = (gh * fb[:, tail_of(j)]).astype(BF16)
            gate_acc[...] += dot_nt(gg, pg[:, tail_of(j)])
            up_acc[...] += dot_nt(gu, pu[:, tail_of(j)])
            return carry

        lax.fori_loop(0, ff // TAIL, body, 0)

    def reduce_copy(i, src, dst, target, source):
        return pltpu.make_async_remote_copy(
            src_ref=src.at[pl.ds(pl.multiple_of(target * part, part), part)],
            dst_ref=dst.at[source],
            send_sem=s_rs.at[i, target], recv_sem=s_rr.at[i, source],
            device_id={"tensor": target}, device_id_type=MESH,
        )

    def nothing():
        pass

    def f_xo1():
        @pl.when(pos == 0)
        def _():
            go_near(xo[1])

    def f_a0():
        go_x(a[0])

        @pl.when(at1)
        def _():
            go_up(a[0])

    def f_a1():
        @pl.when(at1)
        def _():
            go_up(a[1])

    def f_b0():
        go_x(b[0])

        @pl.when(at1)
        def _():
            go_near(b[0])

    def f_b1():
        @pl.when(at1)
        def _():
            go_near(b[1])

        @pl.when(pos == 0)
        def _():
            go_x(b[1])

    def f_c0():
        go_x(c[0])

        @pl.when(at1)
        def _():
            go_near(c[0])

    def f_c1():
        go_x(c[1])

        @pl.when(at1)
        def _():
            go_near(c[1])
            go_near(xo[1])
            go_up(xo[1])

    def f_last():
        for d in range(1, n):
            reduce_copy(0, send0, red0, (me + d) % n, me).start()

    order = [
        (own[0], None), (own[1], None),
        (xo[0], nothing), (a[0], f_a0), (xo[1], f_xo1), (a[1], f_a1), (b[0], f_b0),
        (xa[0], nothing), (b[1], f_b1), (c[0], f_c0), (xb[0], nothing), (c[1], f_c1),
        (xb[1], nothing), (xc[0], nothing), (xa[1], nothing), (xc[1], f_last),
    ]
    steps = len(order)
    for i, (slot, forward) in enumerate(order):
        if i + 1 < steps:
            w_copy(order[i + 1][0], (i + 1) % 2).start()
        if forward is not None:
            piece(slot, 0, to_x).wait_recv()
            forward()
        w_copy(slot, i % 2).wait()
        if i + 1 < steps:
            matmul(slot, i % 2, i == 0)
        else:
            last(slot, i % 2)

    send1[...] = jnp.concatenate([gate_acc[...], up_acc[...]], axis=1)
    for d in range(1, n):
        reduce_copy(1, send1, red1, (me + d) % n, me).start()
    mine = pl.ds(pl.multiple_of(me * part, part), part)
    sum0, sum1 = send0[mine, :], send1[mine, :]
    for d in range(1, n):
        src = (me + d) % n
        reduce_copy(0, send0, red0, src, src).wait_recv()
        sum0 = sum0 + red0[src]
    for d in range(1, n):
        src = (me + d) % n
        reduce_copy(1, send1, red1, src, src).wait_recv()
        sum1 = sum1 + red1[src]
    seq = ids_ref.shape[1]
    per = seq // part
    ids = jnp.broadcast_to(ids_ref[pl.ds(me // per, 1), :], (part, seq))
    row = lax.broadcasted_iota(jnp.int32, (part, seq), 0) + (me % per) * part
    at = row == lax.broadcasted_iota(jnp.int32, (part, seq), 1)
    mask = jnp.sum(jnp.where(at & (ids != 0), 1.0, 0.0), axis=1, keepdims=True)
    masked = sum0 * mask
    sk[me, 0:64, :] = dot_tn(masked[:, 0:64], sum1)
    sk[me, 64:128, :] = dot_tn(masked[:, 128:192], sum0[:, 0:128])

    def sketch_copy(target, source):
        return pltpu.make_async_remote_copy(
            src_ref=sk.at[source], dst_ref=sk.at[source],
            send_sem=s_ss.at[target], recv_sem=s_sr.at[source],
            device_id={"tensor": target}, device_id_type=MESH,
        )

    for d in range(1, n):
        sketch_copy((me + d) % n, me).start()
    for slot in own + [a[0], c[0], c[1], b[0]]:
        piece(slot, 0, to_x).wait_send()
    for slot in own:
        piece(slot, 1, to_near).wait_send()

    @pl.when(pos == 0)
    def _():
        piece(b[1], 0, to_x).wait_send()
        piece(xo[1], 1, to_near).wait_send()

    @pl.when(at1)
    def _():
        for slot in own + [a[0], a[1], xo[1]]:
            piece(slot, 2, to_up).wait_send()
        for slot in [b[0], b[1], c[0], c[1], xo[1]]:
            piece(slot, 1, to_near).wait_send()

    for d in range(1, n):
        t = (me + d) % n
        reduce_copy(0, send0, red0, t, me).wait_send()
        reduce_copy(1, send1, red1, t, me).wait_send()
    for d in range(1, n):
        t = (me + d) % n
        sketch_copy(t, t).wait_recv()
    for d in range(1, n):
        sketch_copy((me + d) % n, me).wait_send()
    out_ref[...] = sk[...]


def fused(x_act, gate_pre, up_pre, out_grad, down_weight, pi, pg, pu, ph, po, ids):
    rows, feat = x_act.shape
    ff = gate_pre.shape[1]
    half = feat // 2
    n = 8
    rank = pi.shape[0]
    part = rows // n
    dma = pltpu.SemaphoreType.DMA
    vm = pltpu.VMEM
    any_spec = pl.BlockSpec(memory_space=pl.ANY)
    return pl.pallas_call(
        fused_kernel,
        out_shape=jax.ShapeDtypeStruct((n, 2 * rank, 2 * rank), F32),
        in_specs=[any_spec] * 10 + [pl.BlockSpec(memory_space=pltpu.VMEM)],
        out_specs=pl.BlockSpec(memory_space=pltpu.VMEM),
        scratch_shapes=[
            vm((2 * n, rows, half), BF16),
            vm((rows, ff), F32),
            vm((rows, ff), F32),
            vm((rows, ff), F32),
            vm((2, ff, half), BF16),
            vm((2, rows, TILE), BF16),
            vm((2, rows, TILE), BF16),
            vm((rank, feat), BF16),
            vm((rank, ff), BF16),
            vm((rank, ff), BF16),
            vm((rank, ff), BF16),
            vm((rank, feat), BF16),
            vm((rows, rank), F32),
            vm((rows, rank), F32),
            vm((rows, rank), F32),
            vm((rows, 4 * rank), F32),
            vm((rows, 2 * rank), F32),
            vm((n, part, 4 * rank), F32),
            vm((n, part, 2 * rank), F32),
            vm((n, 2 * rank, 2 * rank), F32),
            dma((2 * n, 3)), dma((2 * n,)), dma((2,)), dma((2,)), dma((2,)), dma((2,)), dma((2,)),
            dma((5,)), dma((2, n)), dma((2, n)), dma((n,)), dma((n,)),
        ],
        compiler_params=pltpu.CompilerParams(
            collective_id=0, has_side_effects=True, vmem_limit_bytes=VLIM
        ),
        cost_estimate=pl.CostEstimate(
            flops=2 * rows * ff * feat * n, bytes_accessed=2 * ff * feat * n, transcendentals=rows * ff
        ),
    )(x_act, gate_pre, up_pre, out_grad, down_weight, pi, pg, pu, ph, po, ids)


VLIM = 66 * 1000 * 1000


def tail(sketch, target_sketch, source_label):
    highest = lax.Precision.HIGHEST
    inv_norm = lax.rsqrt(jnp.mean(sketch * sketch, axis=1, keepdims=True) + 1e-06)
    unit = sketch * inv_norm
    scores = jnp.dot(unit, target_sketch.astype(F32).T, precision=highest) / jnp.sqrt(
        F32(sketch.shape[1])
    )
    onehot = (source_label[:, None] == jnp.arange(NSRC, dtype=jnp.int32)[None, :]).astype(F32)
    local_totals = jnp.dot(onehot.T, scores, precision=highest)
    local_counts = jnp.sum(onehot, axis=0)
    totals, counts = lax.psum((local_totals, local_counts), "dp")
    source_scores = totals / jnp.maximum(counts, 1.0)[:, None]
    return (scores, source_scores)


def local_fused(
    x_act, gate_pre, up_pre, out_grad, down_weight, proj_input, proj_gate, proj_up, proj_hidden,
    proj_output, target_sketch, token_ids, source_label,
):
    cands = token_ids.shape[0]
    r = proj_input.shape[1]
    parts = fused(
        x_act, gate_pre, up_pre, out_grad, down_weight,
        proj_input.T, proj_gate.T, proj_up.T, proj_hidden.T, proj_output.T, token_ids,
    )
    mats = parts.reshape(cands, 8 // cands, 2 * r, 2 * r).sum(axis=1)
    sketch = jnp.concatenate(
        [
            mats[:, :r, :r].reshape(cands, r * r),
            mats[:, :r, r:].reshape(cands, r * r),
            mats[:, r:, r:].reshape(cands, r * r),
        ],
        axis=1,
    )
    return tail(sketch, target_sketch, source_label)


def local(
    x_act,
    gate_pre,
    up_pre,
    out_grad,
    down_weight,
    proj_input,
    proj_gate,
    proj_up,
    proj_hidden,
    proj_output,
    target_sketch,
    token_ids,
    source_label,
):
    tok_rows = x_act.shape[0]
    cands, seq_len = token_ids.shape
    rank = proj_input.shape[1]
    highest = lax.Precision.HIGHEST
    grad_hidden = lax.dot_general(
        lax.all_gather(out_grad, "tensor", axis=1, tiled=True),
        down_weight,
        (((1,), (1,)), ((), ())),
        preferred_element_type=jnp.float32,
    )
    gval = gate_pre.astype(jnp.float32)
    uval = up_pre.astype(jnp.float32)
    sig = jax.nn.sigmoid(gval)
    hidden = (gval * sig * uval).astype(jnp.bfloat16)
    grad_gate = (grad_hidden * uval * sig * (1.0 + gval * (1.0 - sig))).astype(jnp.bfloat16)
    grad_up = (grad_hidden * gval * sig).astype(jnp.bfloat16)
    mask = (token_ids != 0).astype(jnp.float32).reshape(tok_rows)
    term_in = dotf(x_act, proj_input)
    term_gate = dotf(grad_gate, proj_gate)
    term_up = dotf(grad_up, proj_up)
    term_hid = dotf(hidden, proj_hidden)
    term_out = dotf(out_grad, proj_output)
    whole = lax.psum((term_in, term_gate, term_up, term_hid, term_out), "tensor")
    p_in = (whole[0] * mask[:, None]).reshape(cands, seq_len, rank)
    p_gate = whole[1].reshape(cands, seq_len, rank)
    p_up = whole[2].reshape(cands, seq_len, rank)
    p_hid = (whole[3] * mask[:, None]).reshape(cands, seq_len, rank)
    p_out = whole[4].reshape(cands, seq_len, rank)
    first = jnp.einsum("csi,csj->cij", p_in, p_gate, precision=highest)
    second = jnp.einsum("csi,csj->cij", p_in, p_up, precision=highest)
    third = jnp.einsum("csi,csj->cij", p_hid, p_out, precision=highest)
    sketch = jnp.concatenate(
        [
            first.reshape(cands, rank * rank),
            second.reshape(cands, rank * rank),
            third.reshape(cands, rank * rank),
        ],
        axis=1,
    )
    return tail(sketch, target_sketch, source_label)


def solution(mesh):
    in_specs = (
        P(("groups", "dp"), "tensor"),
        P(("groups", "dp"), "tensor"),
        P(("groups", "dp"), "tensor"),
        P(("groups", "dp"), "tensor"),
        P("tensor", None),
        P("tensor", None),
        P("tensor", None),
        P("tensor", None),
        P("tensor", None),
        P("tensor", None),
        P(("groups", "tensor"), None),
        P(("groups", "dp"), None),
        P(("groups", "dp")),
    )
    out_specs = (P(("groups", "dp"), "tensor"), P("groups", "tensor"))
    body = local_fused if mesh.shape["tensor"] == 8 else local
    return jax.shard_map(body, mesh=mesh, in_specs=in_specs, out_specs=out_specs, check_vma=False)
```
